32 devices in a mesh: expert: 2 (over x), row: 4 (over z), col: 4 (over y, core).
Axes of the slice: x: 2, y: 2, z: 4, core: 2. Of those that a mesh axis runs over, the one named last changes fastest.
Arguments:
- tokens: bfloat16 [2048, 3584], P(('expert', 'col'), 'row'), may hold values from -6 to 6
- slots: int32 [8, 6, 2, 2], P(('expert', 'col')), may hold values from 0 to 255
- counts: int32 [6, 2], replicated, may hold values from 1 to 16, as said below
- owner: int32 [2], replicated, may hold values from 0 to 1, each once
Outputs:
- moments: float32 [2, 3584, 3584], P('expert', 'row', 'col')
The draws below stay inside these ranges and needn't reach their ends.
Inputs may be any that keep to these rules, and one draw needn't show every extreme that they name: `counts`: in every panel at least one expert's count is 16.
All inputs are finite; a program needn't handle non-finite values.
Results may differ from the reference program's by a relative error of at most 0.0003.
Values may be sent and summed in bfloat16 or wider, within the bound.
A program may use at most 64 MiB of HBM per device.

```python
import jax
import jax.numpy as jnp
from jax import lax

W = 3584
SLOT = 2
TOK_DEV = 256
PANELS = 6
EXPERTS = 2
PANEL_ROWS = 16
TOKENS = 2048
N_EXPERT = 2
N_COL = 4


def draw_counts(key, part):
    first_key = jax.random.fold_in(key, 11)
    second_key = jax.random.fold_in(key, 23)
    base_counts = jax.random.randint(first_key, (PANELS, EXPERTS), 1, PANEL_ROWS + 1)
    hottest = jax.random.randint(second_key, (PANELS,), 0, EXPERTS)
    column = jnp.arange(EXPERTS, dtype=jnp.int32)[None, :]
    return jnp.where(column == hottest[:, None], PANEL_ROWS, base_counts).astype(jnp.int32)


def touch_ends(result, own_key, smallest, high):
    shape = result.shape
    spot = [jax.random.randint(jax.random.fold_in(own_key, axis), (), 0, shape[axis]) for axis in range(len(shape))]
    result = result.at[tuple(spot)].set(smallest)
    longest = shape.index(max(shape))
    spot[longest] = (spot[longest] + 1) % shape[longest]
    return result.at[tuple(spot)].set(high)


def levels(rng, extent, shards, low, top_value):
    level, own = 1.0, jax.random.fold_in(rng, 6)
    for dim, parts in shards:
        heights = jnp.exp(jax.random.uniform(jax.random.fold_in(own, dim), (parts,), jnp.float32, low / len(shards), top_value / len(shards)))
        level = level * jnp.repeat(heights, extent[dim] // parts).reshape([-1 if axis == dim else 1 for axis in range(len(extent))])
    return level


def noise(own_key, extent, deviation, bound, cuts=(), held_as=jnp.bfloat16):
    entries = deviation * jax.random.normal(own_key, extent, jnp.float32)
    if cuts:
        entries = entries * levels(own_key, extent, cuts, -0.22, 0.18)
    return jnp.clip(entries, -bound, bound).astype(held_as)


def setup_inputs(seed: int = 0) -> dict:
    key_of = jax.random.split(jax.random.key(seed), 5)
    tokens = noise(key_of[0], (TOKENS, W), 1.0, 6.0, ((0, 8), (1, 4)))
    slots = touch_ends(jax.random.randint(key_of[1], (N_EXPERT * N_COL, PANELS, EXPERTS, SLOT), 0, TOK_DEV), jax.random.fold_in(key_of[1], 1), 0, TOK_DEV - 1).astype(jnp.int32)
    counts = draw_counts(jax.random.fold_in(key_of[4], 71), 0)
    owner = jax.random.permutation(key_of[3], EXPERTS).astype(jnp.int32)
    return {"tokens": tokens, "slots": slots, "counts": counts, "owner": owner}


def reference(tokens, slots, counts, owner):
    inverse = jnp.argsort(owner).astype(jnp.int32)

    def one_group(group):
        expert_id = inverse[group]
        local = jnp.take(slots, expert_id, axis=2)
        local = jnp.transpose(local, (1, 0, 2)).reshape(PANELS, PANEL_ROWS)
        position = jnp.arange(PANEL_ROWS, dtype=jnp.int32)
        global_rows = ((position // SLOT) * TOK_DEV)[None, :] + local
        usable = position[None, :] < jnp.take(counts, expert_id, axis=1)[:, None]
        picked = tokens[global_rows.reshape(-1).astype(jnp.int32)]
        picked = jnp.where(usable.reshape(-1)[:, None], picked, jnp.zeros_like(picked))
        moment = jnp.dot(picked.T, picked, preferred_element_type=jnp.float32)
        row_total = jnp.sum(jnp.take(counts, expert_id, axis=1)).astype(jnp.float32)
        return moment / row_total

    return lax.map(one_group, jnp.arange(EXPERTS, dtype=jnp.int32))
```

```python
import functools

import jax
import jax.numpy as jnp
from jax import lax
from jax.experimental import pallas as pl
from jax.experimental.pallas import tpu as pltpu
from jax.sharding import PartitionSpec as P

MESH = pl.DeviceIdType.MESH


def each(count, body):
    if count <= 4:
        for i in range(count):
            body(i)
    else:
        pl.loop(0, count)(body)


def wrap(index, count):
    return lax.rem(index + count, count)


def expert_of(owner_ref, group, expert_count):
    found = jnp.int32(0)
    for e in range(expert_count):
        found = jnp.where(owner_ref[e] == group, jnp.int32(e), found)
    return found


def exchange(sizes, owner_ref, counts_ref, slots_ref, tokens_ref, buf, tokens, picked, token_sem, own_sem, send_sem, recv_sem):
    n_group, n_row, n_col = sizes
    block_tokens, features = tokens_ref.shape
    panels, experts = counts_ref.shape
    slot_count = slots_ref.shape[3]
    padded = picked.shape[1]
    x, r, c = lax.axis_index("expert"), lax.axis_index("row"), lax.axis_index("col")
    block = x * n_col + c

    load = pltpu.make_async_copy(tokens_ref, tokens, token_sem)
    load.start()

    barrier = pltpu.get_barrier_semaphore()

    def greet(row, first_group, first_col):
        def per_group(dg):
            group = wrap(x + dg, n_group)
            for dc in range(n_col):
                def signal(group=group, dc=dc):
                    pl.semaphore_signal(
                        barrier, inc=1, device_id=(group, row, wrap(c + dc, n_col)), device_id_type=MESH
                    )
                if first_col and dc == 0:
                    pl.when(group != x)(signal)
                else:
                    signal()
        each(n_group, per_group)

    greet(r, 0, True)

    @pl.when(r != c)
    def _():
        greet(c, 0, False)

    load.wait()
    rows_iota = lax.broadcasted_iota(jnp.int32, (padded, block_tokens), 0)
    token_iota = lax.broadcasted_iota(jnp.int32, (padded, block_tokens), 1)

    def pick(dg):
        group = wrap(x + dg, n_group)
        e = expert_of(owner_ref, group, experts)
        index = jnp.full((padded, block_tokens), -1, jnp.int32)
        for k in range(panels):
            count = counts_ref[k, e]
            for j in range(slot_count):
                slot = jnp.where(block * slot_count + j < count, slots_ref[0, k, e, j], jnp.int32(-1))
                index = jnp.where(rows_iota == k * slot_count + j, slot, index)
        onehot = (index == token_iota).astype(jnp.bfloat16)
        picked[group] = jnp.dot(onehot, tokens[...], preferred_element_type=jnp.float32).astype(jnp.bfloat16)

    each(n_group, pick)
    pl.semaphore_wait(barrier, n_group * (n_row - 1) + n_group * n_col - 1)

    own = pltpu.make_async_copy(picked.at[x], buf.at[0, block], own_sem)

    def right_copy(dg, dr):
        group = wrap(x + dg, n_group)
        return pltpu.make_async_remote_copy(
            src_ref=picked.at[group],
            dst_ref=buf.at[1, block],
            send_sem=send_sem.at[1, dg, dr],
            recv_sem=recv_sem.at[1, block],
            device_id=(group, wrap(r + dr, n_row), r),
            device_id_type=MESH,
        )

    def left_copy(dg, dc):
        group = wrap(x + dg, n_group)
        return pltpu.make_async_remote_copy(
            src_ref=picked.at[group],
            dst_ref=buf.at[0, block],
            send_sem=send_sem.at[0, dg, dc],
            recv_sem=recv_sem.at[0, block],
            device_id=(group, r, wrap(c + dc, n_col)),
            device_id_type=MESH,
        )

    def all_copies(act):
        def right(dg):
            for dr in range(1, n_row):
                act(right_copy(dg, dr))

        def left(dg):
            for dc in range(n_col):
                if dc > 0:
                    act(left_copy(dg, dc))
                elif isinstance(dg, int):
                    if dg > 0:
                        act(left_copy(dg, dc))
                else:
                    pl.when(dg > 0)(lambda: act(left_copy(dg, 0)))

        each(n_group, right)
        each(n_group, left)

    all_copies(lambda copy: copy.start())
    own.start()

    def arrived(side, b):
        pltpu.make_async_remote_copy(
            src_ref=picked.at[0],
            dst_ref=buf.at[side, b],
            send_sem=send_sem.at[0, 0, 0],
            recv_sem=recv_sem.at[side, b],
            device_id=(x, r, c),
            device_id_type=MESH,
        ).wait_recv()

    def wait_left(dg):
        for dc in range(n_col):
            b = wrap(x + dg, n_group) * n_col + wrap(c + dc, n_col)
            if dc > 0:
                arrived(0, b)
            elif isinstance(dg, int):
                if dg > 0:
                    arrived(0, b)
            else:
                pl.when(dg > 0)(lambda: arrived(0, b))

    def wait_right(dg):
        for dc in range(n_col):
            arrived(1, wrap(x + dg, n_group) * n_col + dc)

    own.wait()
    all_copies(lambda copy: copy.wait_send())
    each(n_group, wait_left)

    @pl.when(r != c)
    def _():
        each(n_group, wait_right)


def multiply(tile, owner_ref, counts_ref, rows_ref, out_ref, product, sems):
    panels, experts = counts_ref.shape
    features = rows_ref.shape[-1]
    x, r, c = lax.axis_index("expert"), lax.axis_index("row"), lax.axis_index("col")
    e = expert_of(owner_ref, x, experts)
    total = jnp.int32(0)
    for k in range(panels):
        total = total + counts_ref[k, e]
    scale = 1.0 / jnp.full((1, features), total, jnp.int32).astype(jnp.float32)
    side = jnp.where(r == c, 0, 1)
    right = rows_ref[side].reshape(-1, features)
    copies = []
    for t in range(features // tile):
        span = pl.ds(t * tile, tile)
        left = rows_ref[0, :, :, span].reshape(-1, tile)
        part = lax.dot_general(left, right, (((0,), (0,)), ((), ())), preferred_element_type=jnp.float32)
        product[span, :] = part * scale
        copy = pltpu.make_async_copy(product.at[span, :], out_ref.at[0, span, :], sems.at[t])
        copy.start()
        copies.append(copy)
    for copy in copies:
        copy.wait()


def per_device(tokens, slots, counts, owner):
    n_group, n_row, n_col = lax.axis_size("expert"), lax.axis_size("row"), lax.axis_size("col")
    block_tokens, features = tokens.shape
    panels, slot_count = counts.shape[0], slots.shape[3]
    padded = -(-panels * slot_count // 16) * 16
    blocks = n_group * n_col
    smem = pl.BlockSpec(memory_space=pltpu.SMEM)
    rows = pl.pallas_call(
        functools.partial(exchange, (n_group, n_row, n_col)),
        out_shape=jax.ShapeDtypeStruct((2, blocks, padded, features), tokens.dtype),
        in_specs=[smem, smem, smem, pl.BlockSpec(memory_space=pl.ANY)],
        out_specs=pl.BlockSpec(memory_space=pltpu.VMEM),
        scratch_shapes=[
            pltpu.VMEM((block_tokens, features), tokens.dtype),
            pltpu.VMEM((n_group, padded, features), tokens.dtype),
            pltpu.SemaphoreType.DMA,
            pltpu.SemaphoreType.DMA,
            pltpu.SemaphoreType.DMA((2, n_group, max(n_row, n_col))),
            pltpu.SemaphoreType.DMA((2, blocks)),
        ],
        compiler_params=pltpu.CompilerParams(
            collective_id=0, has_side_effects=True, vmem_limit_bytes=32 * 1024 * 1024
        ),
    )(owner, counts, slots, tokens)
    tile = 128
    return pl.pallas_call(
        functools.partial(multiply, tile),
        out_shape=jax.ShapeDtypeStruct((1, features, features), jnp.float32),
        in_specs=[smem, smem, pl.BlockSpec(memory_space=pltpu.VMEM)],
        out_specs=pl.BlockSpec(memory_space=pl.ANY),
        scratch_shapes=[
            pltpu.VMEM((features, features), jnp.float32),
            pltpu.SemaphoreType.DMA((features // tile,)),
        ],
        compiler_params=pltpu.CompilerParams(vmem_limit_bytes=32 * 1024 * 1024),
    )(owner, counts, rows)


def solution(mesh):
    return jax.shard_map(
        per_device,
        mesh=mesh,
        in_specs=(P(("expert", "col"), "row"), P(("expert", "col"), None, None, None), P(), P()),
        out_specs=P("expert", "row", "col"),
        check_vma=False,
    )
```

```python
import functools

import jax
import jax.numpy as jnp
from jax import lax
from jax.experimental import pallas as pl
from jax.experimental.pallas import tpu as pltpu
from jax.sharding import PartitionSpec as P

MESH = pl.DeviceIdType.MESH


def each(count, body):
    if count <= 4:
        for i in range(count):
            body(i)
    else:
        pl.loop(0, count)(body)


def wrap(index, count):
    return lax.rem(index + count, count)


def expert_of(owner_ref, group, expert_count):
    found = jnp.int32(0)
    for e in range(expert_count):
        found = jnp.where(owner_ref[e] == group, jnp.int32(e), found)
    return found


def exchange(
    sizes, tile, owner_hbm, counts_hbm, slots_hbm, tokens_hbm, out_ref,
    owner_ref, counts_ref, slots_ref, tokens, picked, buf, load_sem, own_sem, send_sem, recv_sem,
):
    n_group, n_row, n_col = sizes
    block_tokens, features = tokens.shape
    experts, panels = counts_ref.shape
    slot_count = slots_ref.shape[2]
    padded = picked.shape[1]
    x, r, c = lax.axis_index("expert"), lax.axis_index("row"), lax.axis_index("col")
    block = x * n_col + c

    loads = [
        pltpu.make_async_copy(source, target, load_sem.at[i])
        for i, (source, target) in enumerate(
            [(tokens_hbm, tokens), (slots_hbm, slots_ref), (counts_hbm, counts_ref), (owner_hbm, owner_ref)]
        )
    ]
    for load in loads:
        load.start()

    barrier = pltpu.get_barrier_semaphore()

    def greet(row, first_group, first_col):
        def per_group(dg):
            group = wrap(x + dg, n_group)
            for dc in range(n_col):
                def signal(group=group, dc=dc):
                    pl.semaphore_signal(
                        barrier, inc=1, device_id=(group, row, wrap(c + dc, n_col)), device_id_type=MESH
                    )
                if first_col and dc == 0:
                    pl.when(group != x)(signal)
                else:
                    signal()
        each(n_group, per_group)

    greet(r, 0, True)

    @pl.when(r != c)
    def _():
        greet(c, 0, False)

    for load in loads:
        load.wait()
    rows_iota = lax.broadcasted_iota(jnp.int32, (padded, block_tokens), 0)
    token_iota = lax.broadcasted_iota(jnp.int32, (padded, block_tokens), 1)

    def pick(dg):
        group = wrap(x + dg, n_group)
        e = expert_of(owner_ref, group, experts)
        index = jnp.full((padded, block_tokens), -1, jnp.int32)
        for k in range(panels):
            count = counts_ref[e, k]
            for j in range(slot_count):
                slot = jnp.where(block * slot_count + j < count, slots_ref[0, e, j, k], jnp.int32(-1))
                index = jnp.where(rows_iota == k * slot_count + j, slot, index)
        onehot = (index == token_iota).astype(jnp.bfloat16)
        picked[group] = jnp.dot(onehot, tokens[...], preferred_element_type=jnp.float32).astype(jnp.bfloat16)

    each(n_group, pick)
    pl.semaphore_wait(barrier, n_group * (n_row - 1) + n_group * n_col - 1)

    own = pltpu.make_async_copy(picked.at[x], buf.at[0, block], own_sem)

    def right_copy(dg, dr):
        group = wrap(x + dg, n_group)
        return pltpu.make_async_remote_copy(
            src_ref=picked.at[group],
            dst_ref=buf.at[1, block],
            send_sem=send_sem.at[1, dg, dr],
            recv_sem=recv_sem.at[1, block],
            device_id=(group, wrap(r + dr, n_row), r),
            device_id_type=MESH,
        )

    def left_copy(dg, dc):
        group = wrap(x + dg, n_group)
        return pltpu.make_async_remote_copy(
            src_ref=picked.at[group],
            dst_ref=buf.at[0, block],
            send_sem=send_sem.at[0, dg, dc],
            recv_sem=recv_sem.at[0, block],
            device_id=(group, r, wrap(c + dc, n_col)),
            device_id_type=MESH,
        )

    def all_copies(act):
        def right(dg):
            for dr in range(1, n_row):
                act(right_copy(dg, dr))

        def left(dg):
            for dc in range(n_col):
                if dc > 0:
                    act(left_copy(dg, dc))
                elif isinstance(dg, int):
                    if dg > 0:
                        act(left_copy(dg, dc))
                else:
                    pl.when(dg > 0)(lambda: act(left_copy(dg, 0)))

        each(n_group, right)
        each(n_group, left)

    all_copies(lambda copy: copy.start())
    own.start()

    def arrived(side, b):
        pltpu.make_async_remote_copy(
            src_ref=picked.at[0],
            dst_ref=buf.at[side, b],
            send_sem=send_sem.at[0, 0, 0],
            recv_sem=recv_sem.at[side, b],
            device_id=(x, r, c),
            device_id_type=MESH,
        ).wait_recv()

    def wait_left(dg):
        for dc in range(n_col):
            b = wrap(x + dg, n_group) * n_col + wrap(c + dc, n_col)
            if dc > 0:
                arrived(0, b)
            elif isinstance(dg, int):
                if dg > 0:
                    arrived(0, b)
            else:
                pl.when(dg > 0)(lambda: arrived(0, b))

    def wait_right(dg):
        for dc in range(n_col):
            arrived(1, wrap(x + dg, n_group) * n_col + dc)

    own.wait()
    all_copies(lambda copy: copy.wait_send())
    each(n_group, wait_left)

    @pl.when(r != c)
    def _():
        each(n_group, wait_right)

    e = expert_of(owner_ref, x, experts)
    total = jnp.int32(0)
    for k in range(panels):
        total = total + counts_ref[e, k]
    scale = 1.0 / jnp.full((1, features), total, jnp.int32).astype(jnp.float32)
    right_rows = buf[jnp.where(r == c, 0, 1)].reshape(-1, features)
    for t in range(features // tile):
        span = pl.ds(t * tile, tile)
        left_rows = buf[0, :, :, span].reshape(-1, tile)
        part = lax.dot_general(left_rows, right_rows, (((0,), (0,)), ((), ())), preferred_element_type=jnp.float32)
        out_ref[0, span, :] = part * scale


def per_device(tokens, slots, counts, owner):
    n_group, n_row, n_col = lax.axis_size("expert"), lax.axis_size("row"), lax.axis_size("col")
    block_tokens, features = tokens.shape
    panels, slot_count = counts.shape[0], slots.shape[3]
    padded = -(-panels * slot_count // 16) * 16
    blocks = n_group * n_col
    counts = counts.T
    slots = jnp.transpose(slots, (0, 2, 3, 1))
    hbm = pl.BlockSpec(memory_space=pltpu.HBM)
    return pl.pallas_call(
        functools.partial(exchange, (n_group, n_row, n_col), 128),
        out_shape=jax.ShapeDtypeStruct((1, features, features), jnp.float32),
        in_specs=[hbm, hbm, hbm, hbm],
        out_specs=pl.BlockSpec(memory_space=pltpu.VMEM),
        scratch_shapes=[
            pltpu.SMEM(owner.shape, jnp.int32),
            pltpu.SMEM(counts.shape, jnp.int32),
            pltpu.SMEM(slots.shape, jnp.int32),
            pltpu.VMEM((block_tokens, features), tokens.dtype),
            pltpu.VMEM((n_group, padded, features), tokens.dtype),
            pltpu.VMEM((2, blocks, padded, features), tokens.dtype),
            pltpu.SemaphoreType.DMA((4,)),
            pltpu.SemaphoreType.DMA,
            pltpu.SemaphoreType.DMA((2, n_group, max(n_row, n_col))),
            pltpu.SemaphoreType.DMA((2, blocks)),
        ],
        compiler_params=pltpu.CompilerParams(
            collective_id=0, has_side_effects=True, vmem_limit_bytes=32 * 1024 * 1024
        ),
    )(*[pltpu.with_memory_space_constraint(a, pltpu.HBM) for a in (owner, counts, slots, tokens)])


def solution(mesh):
    return jax.shard_map(
        per_device,
        mesh=mesh,
        in_specs=(P(("expert", "col"), "row"), P(("expert", "col"), None, None, None), P(), P()),
        out_specs=P("expert", "row", "col"),
        check_vma=False,
    )
```

```python
import functools

import jax
import jax.numpy as jnp
from jax import lax
from jax.experimental import pallas as pl
from jax.experimental.pallas import tpu as pltpu
from jax.sharding import PartitionSpec as P

MESH = pl.DeviceIdType.MESH


def each(count, body):
    if count <= 4:
        for i in range(count):
            body(i)
    else:
        pl.loop(0, count)(body)


def unless_self(dg, dc, act):
    if dc > 0 or (isinstance(dg, int) and dg > 0):
        act()
    elif not isinstance(dg, int):
        pl.when(dg > 0)(act)


def wrap(index, count):
    return lax.rem(index + count, count)


def expert_of(owner_ref, group, expert_count):
    found = jnp.int32(0)
    for e in range(expert_count):
        found = jnp.where(owner_ref[e] == group, jnp.int32(e), found)
    return found


def exchange(
    sizes, tile, owner_hbm, counts_hbm, slots_hbm, tokens_hbm, out_ref,
    owner_ref, counts_ref, slots_ref, tokens, picked, packed, landed, buf,
    load_sem, own_sem, line_send, line_recv, send_sem, recv_sem,
):
    n_group, n_row, n_col = sizes
    block_tokens, features = tokens.shape
    experts, panels = counts_ref.shape
    slot_count = slots_ref.shape[2]
    per_group = panels * slot_count
    tiles = picked.shape[1]
    x, r, c = lax.axis_index("expert"), lax.axis_index("row"), lax.axis_index("col")
    block = x * n_col + c

    loads = [
        pltpu.make_async_copy(source, target, load_sem.at[i])
        for i, (source, target) in enumerate(
            [(tokens_hbm, tokens), (slots_hbm, slots_ref), (counts_hbm, counts_ref), (owner_hbm, owner_ref)]
        )
    ]
    for load in loads:
        load.start()

    barrier = pltpu.get_barrier_semaphore()

    def greet(dg):
        for dc in range(n_col):
            def signal(dc=dc):
                pl.semaphore_signal(
                    barrier, inc=1, device_id=(wrap(x + dg, n_group), r, wrap(c + dc, n_col)), device_id_type=MESH
                )
            unless_self(dg, dc, signal)

    for dr in range(1, n_row):
        pl.semaphore_signal(barrier, inc=1, device_id=(x, wrap(r + dr, n_row), c), device_id_type=MESH)
    each(n_group, greet)

    for load in loads:
        load.wait()
    rows_iota = lax.broadcasted_iota(jnp.int32, (tiles * 8, block_tokens), 0)
    token_iota = lax.broadcasted_iota(jnp.int32, (tiles * 8, block_tokens), 1)
    packed[...] = jnp.zeros_like(packed)

    def first_tile(group):
        return (group * per_group) // 8

    def pick(group):
        e = expert_of(owner_ref, group, experts)
        skipped = group * per_group - first_tile(group) * 8
        index = jnp.full((tiles * 8, block_tokens), -1, jnp.int32)
        for k in range(panels):
            count = counts_ref[e, k]
            for j in range(slot_count):
                slot = jnp.where(block * slot_count + j < count, slots_ref[0, e, j, k], jnp.int32(-1))
                index = jnp.where(rows_iota == k * slot_count + j + skipped, slot, index)
        onehot = (index == token_iota).astype(jnp.bfloat16)
        rows = jnp.dot(onehot, tokens[...], preferred_element_type=jnp.float32)
        rows = rows.reshape(tiles, 8, features).astype(jnp.bfloat16)
        picked[group] = rows
        window = pl.ds(first_tile(group), tiles)
        packed[window] = packed[window] + rows

    each(n_group, pick)
    pl.semaphore_wait(barrier, n_row - 1 + n_group * n_col - 1)

    def line_copy(dr):
        return pltpu.make_async_remote_copy(
            src_ref=packed,
            dst_ref=landed.at[dr - 1],
            send_sem=line_send.at[dr - 1],
            recv_sem=line_recv.at[dr - 1],
            device_id=(x, wrap(r + dr, n_row), c),
            device_id_type=MESH,
        )

    def left_copy(dg, dc):
        group = wrap(x + dg, n_group)
        return pltpu.make_async_remote_copy(
            src_ref=picked.at[group],
            dst_ref=buf.at[0, block],
            send_sem=send_sem.at[0, dg, dc],
            recv_sem=recv_sem.at[0, block],
            device_id=(group, r, wrap(c + dc, n_col)),
            device_id_type=MESH,
        )

    def window_of(dr, group):
        return landed.at[dr - 1, pl.ds(first_tile(group), tiles)]

    def right_copy(dr, dg):
        group = wrap(x + dg, n_group)
        return pltpu.make_async_remote_copy(
            src_ref=window_of(dr, group),
            dst_ref=buf.at[1, block],
            send_sem=send_sem.at[1, dg, dr],
            recv_sem=recv_sem.at[1, block],
            device_id=(group, r, wrap(r - dr, n_row)),
            device_id_type=MESH,
        )

    def own_right(dr):
        return pltpu.make_async_copy(window_of(dr, x), buf.at[1, block], own_sem.at[1])

    for dr in range(1, n_row):
        line_copy(dr).start()
    own_left = pltpu.make_async_copy(picked.at[x], buf.at[0, block], own_sem.at[0])
    own_left.start()

    def lefts(act):
        def body(dg):
            for dc in range(n_col):
                unless_self(dg, dc, lambda dc=dc: act(left_copy(dg, dc)))
        each(n_group, body)

    lefts(lambda copy: copy.start())

    def rights(dr, act, act_own):
        here = c == wrap(r - dr, n_row)
        def body(dg):
            if isinstance(dg, int) and dg > 0:
                act(right_copy(dr, dg))
            else:
                pl.when(jnp.logical_or(jnp.logical_not(here), dg != 0))(lambda: act(right_copy(dr, dg)))
        each(n_group, body)
        if act_own is not None:
            pl.when(here)(lambda: act_own(own_right(dr)))

    for dr in range(1, n_row):
        line_copy(dr).wait_recv()
        rights(dr, lambda copy: copy.start(), lambda copy: copy.start())

    def arrived(side, b):
        pltpu.make_async_remote_copy(
            src_ref=picked.at[0],
            dst_ref=buf.at[side, b],
            send_sem=send_sem.at[0, 0, 0],
            recv_sem=recv_sem.at[side, b],
            device_id=(x, r, c),
            device_id_type=MESH,
        ).wait_recv()

    def wait_side(side):
        def body(dg):
            for dc in range(n_col):
                b = wrap(x + dg, n_group) * n_col + wrap(c + dc, n_col)
                unless_self(dg, dc, lambda b=b: arrived(side, b))
        each(n_group, body)

    e = expert_of(owner_ref, x, experts)
    total = jnp.int32(0)
    for k in range(panels):
        total = total + counts_ref[e, k]
    scale = 1.0 / jnp.full((1, features), total, jnp.int32).astype(jnp.float32)

    own_left.wait()
    wait_side(0)

    @pl.when(r != c)
    def _():
        wait_side(1)
        own_right(1).wait()

    right_rows = buf[jnp.where(r == c, 0, 1)].reshape(-1, features)
    for t in range(features // tile):
        span = pl.ds(t * tile, tile)
        left_rows = buf[0, :, :, :, span].reshape(-1, tile)
        part = lax.dot_general(left_rows, right_rows, (((0,), (0,)), ((), ())), preferred_element_type=jnp.float32)
        out_ref[0, span, :] = part * scale

    for dr in range(1, n_row):
        line_copy(dr).wait_send()
        rights(dr, lambda copy: copy.wait_send(), None)
    lefts(lambda copy: copy.wait_send())


def per_device(tokens, slots, counts, owner):
    n_group, n_row, n_col = lax.axis_size("expert"), lax.axis_size("row"), lax.axis_size("col")
    block_tokens, features = tokens.shape
    panels, slot_count = counts.shape[0], slots.shape[3]
    per_group = panels * slot_count
    blocks = n_group * n_col
    starts = [g * per_group for g in range(n_group)]
    tiles = max((g + per_group + 7) // 8 - g // 8 for g in starts)
    packed_tiles = starts[-1] // 8 + tiles
    counts = counts.T
    slots = jnp.transpose(slots, (0, 2, 3, 1))
    hbm = pl.BlockSpec(memory_space=pltpu.HBM)
    return pl.pallas_call(
        functools.partial(exchange, (n_group, n_row, n_col), 128),
        out_shape=jax.ShapeDtypeStruct((1, features, features), jnp.float32),
        in_specs=[hbm, hbm, hbm, hbm],
        out_specs=pl.BlockSpec(memory_space=pltpu.VMEM),
        scratch_shapes=[
            pltpu.SMEM(owner.shape, jnp.int32),
            pltpu.SMEM(counts.shape, jnp.int32),
            pltpu.SMEM(slots.shape, jnp.int32),
            pltpu.VMEM((block_tokens, features), tokens.dtype),
            pltpu.VMEM((n_group, tiles, 8, features), tokens.dtype),
            pltpu.VMEM((packed_tiles, 8, features), tokens.dtype),
            pltpu.VMEM((n_row - 1, packed_tiles, 8, features), tokens.dtype),
            pltpu.VMEM((2, blocks, tiles, 8, features), tokens.dtype),
            pltpu.SemaphoreType.DMA((4,)),
            pltpu.SemaphoreType.DMA((2,)),
            pltpu.SemaphoreType.DMA((n_row - 1,)),
            pltpu.SemaphoreType.DMA((n_row - 1,)),
            pltpu.SemaphoreType.DMA((2, n_group, max(n_row, n_col))),
            pltpu.SemaphoreType.DMA((2, blocks)),
        ],
        compiler_params=pltpu.CompilerParams(
            collective_id=0, has_side_effects=True, vmem_limit_bytes=32 * 1024 * 1024
        ),
    )(*[pltpu.with_memory_space_constraint(a, pltpu.HBM) for a in (owner, counts, slots, tokens)])


def solution(mesh):
    return jax.shard_map(
        per_device,
        mesh=mesh,
        in_specs=(P(("expert", "col"), "row"), P(("expert", "col"), None, None, None), P(), P()),
        out_specs=P("expert", "row", "col"),
        check_vma=False,
    )
```

```python
import functools

import jax
import jax.numpy as jnp
from jax import lax
from jax.experimental import pallas as pl
from jax.experimental.pallas import tpu as pltpu
from jax.sharding import PartitionSpec as P

MESH = pl.DeviceIdType.MESH


def each(count, body):
    if count <= 4:
        for i in range(count):
            body(i)
    else:
        pl.loop(0, count)(body)


def wrap(index, count):
    return lax.rem(index + count, count)


def expert_of(owner_ref, group, expert_count):
    found = jnp.int32(0)
    for e in range(expert_count):
        found = jnp.where(owner_ref[e] == group, jnp.int32(e), found)
    return found


def exchange(
    sizes, tile, owner_hbm, counts_hbm, slots_hbm, tokens_hbm, out_ref,
    owner_ref, counts_ref, slots_ref, tokens, picked, landed, merged, buf,
    load_sem, own_sem, pair_send, pair_recv, send_sem, recv_sem,
):
    n_group, n_row, n_col = sizes
    block_tokens, features = tokens.shape
    experts, panels = counts_ref.shape
    slot_count = slots_ref.shape[2]
    per_group = panels * slot_count
    _, n_handled, tiles = picked.shape[:3]
    n_pair = n_col // 2
    x, r, c = lax.axis_index("expert"), lax.axis_index("row"), lax.axis_index("col")
    block = x * n_col + c
    parity = c % 2
    partner = c + 1 - 2 * parity

    loads = [
        pltpu.make_async_copy(source, target, load_sem.at[i])
        for i, (source, target) in enumerate(
            [(tokens_hbm, tokens), (slots_hbm, slots_ref), (counts_hbm, counts_ref), (owner_hbm, owner_ref)]
        )
    ]
    for load in loads:
        load.start()

    barrier = pltpu.get_barrier_semaphore()

    def signal(device):
        pl.semaphore_signal(barrier, inc=1, device_id=device, device_id_type=MESH)

    def sender_column(pair):
        return 2 * pair + x % 2

    def greet(row, check):
        def body(dg):
            for pair in range(n_pair):
                device = (wrap(x + dg, n_group), row, sender_column(pair))
                if check:
                    pl.when(jnp.logical_or(device[0] != x, device[2] != c))(lambda device=device: signal(device))
                else:
                    signal(device)
        each(n_group, body)

    signal((x, r, partner))
    greet(r, True)

    @pl.when(r != c)
    def _():
        greet(c, False)

    for load in loads:
        load.wait()
    rows_iota = lax.broadcasted_iota(jnp.int32, (tiles * 8, block_tokens), 0)
    token_iota = lax.broadcasted_iota(jnp.int32, (tiles * 8, block_tokens), 1)

    def first_tile(side):
        return side * (per_group // 8)

    skipped = parity * (per_group % 8)

    def onehot(group):
        e = expert_of(owner_ref, group, experts)
        index = jnp.full((tiles * 8, block_tokens), -1, jnp.int32)
        for k in range(panels):
            count = counts_ref[e, k]
            for j in range(slot_count):
                slot = jnp.where(block * slot_count + j < count, slots_ref[0, e, j, k], jnp.int32(-1))
                index = jnp.where(rows_iota == k * slot_count + j + skipped, slot, index)
        return index == token_iota

    def pick(i):
        chosen = jnp.concatenate([onehot(2 * i), onehot(2 * i + 1)], axis=0).astype(jnp.bfloat16)
        rows = jnp.dot(chosen, tokens[...], preferred_element_type=jnp.float32)
        rows = rows.reshape(2, tiles, 8, features).astype(jnp.bfloat16)
        picked[0, i] = rows[0]
        picked[1, i] = rows[1]

    each(n_handled, pick)

    sends = 1 + n_handled * (n_col + n_row - 1)
    own = x % 2 == parity

    @pl.when(own)
    def _():
        pl.semaphore_wait(barrier, sends - 1)

    @pl.when(jnp.logical_not(own))
    def _():
        pl.semaphore_wait(barrier, sends)

    pair_copy = pltpu.make_async_remote_copy(
        src_ref=picked.at[1 - parity],
        dst_ref=landed,
        send_sem=pair_send,
        recv_sem=pair_recv,
        device_id=(x, r, partner),
        device_id_type=MESH,
    )
    pair_copy.start()
    merged[...] = jnp.zeros_like(merged)
    merged[:, pl.ds(first_tile(parity), tiles)] = picked[parity]
    pair_copy.wait_recv()
    window = pl.ds(first_tile(1 - parity), tiles)
    merged[:, window] = merged[:, window] + landed[...]

    my_slot = x * n_pair + c // 2

    def handled(di):
        return wrap(x // 2 + di, n_handled)

    def right_copy(di, dr):
        return pltpu.make_async_remote_copy(
            src_ref=merged.at[handled(di)],
            dst_ref=buf.at[1, my_slot],
            send_sem=send_sem.at[1, di, dr],
            recv_sem=recv_sem.at[1, my_slot],
            device_id=(2 * handled(di) + parity, wrap(r + dr, n_row), r),
            device_id_type=MESH,
        )

    def left_copy(di, dc):
        return pltpu.make_async_remote_copy(
            src_ref=merged.at[handled(di)],
            dst_ref=buf.at[0, my_slot],
            send_sem=send_sem.at[0, di, dc],
            recv_sem=recv_sem.at[0, my_slot],
            device_id=(2 * handled(di) + parity, r, wrap(c + dc, n_col)),
            device_id_type=MESH,
        )

    def rights(act):
        def body(di):
            for dr in range(1, n_row):
                act(right_copy(di, dr))
        each(n_handled, body)

    def lefts(act):
        def body(di):
            for dc in range(1, n_col):
                act(left_copy(di, dc))
            pl.when(2 * handled(di) + parity != x)(lambda: act(left_copy(di, 0)))
        each(n_handled, body)

    own_copy = pltpu.make_async_copy(merged.at[x // 2], buf.at[0, my_slot], own_sem)
    rights(lambda copy: copy.start())
    lefts(lambda copy: copy.start())
    pl.when(own)(own_copy.start)

    def arrived(side, slot):
        pltpu.make_async_remote_copy(
            src_ref=merged.at[0],
            dst_ref=buf.at[side, slot],
            send_sem=pair_send,
            recv_sem=recv_sem.at[side, slot],
            device_id=(x, r, partner),
            device_id_type=MESH,
        ).wait_recv()

    def wait_left(dg):
        group = wrap(x + dg, n_group)
        for pair in range(n_pair):
            sender = sender_column(pair)
            pl.when(jnp.logical_or(group != x, sender != c))(lambda pair=pair: arrived(0, group * n_pair + pair))

    def wait_right(dg):
        for pair in range(n_pair):
            arrived(1, wrap(x + dg, n_group) * n_pair + pair)

    e = expert_of(owner_ref, x, experts)
    total = jnp.int32(0)
    for k in range(panels):
        total = total + counts_ref[e, k]
    scale = 1.0 / jnp.full((1, features), total, jnp.int32).astype(jnp.float32)

    pl.when(own)(own_copy.wait)
    each(n_group, wait_left)

    @pl.when(r != c)
    def _():
        each(n_group, wait_right)

    right_rows = buf[jnp.where(r == c, 0, 1)].reshape(-1, features)
    for t in range(features // tile):
        span = pl.ds(t * tile, tile)
        left_rows = buf[0, :, :, :, span].reshape(-1, tile)
        part = lax.dot_general(left_rows, right_rows, (((0,), (0,)), ((), ())), preferred_element_type=jnp.float32)
        out_ref[0, span, :] = part * scale

    pair_copy.wait_send()
    rights(lambda copy: copy.wait_send())
    lefts(lambda copy: copy.wait_send())


def per_device(tokens, slots, counts, owner):
    n_group, n_row, n_col = lax.axis_size("expert"), lax.axis_size("row"), lax.axis_size("col")
    block_tokens, features = tokens.shape
    panels, slot_count = counts.shape[0], slots.shape[3]
    per_group = panels * slot_count
    n_handled, slots_in = n_group // 2, n_group * n_col // 2
    tiles = (per_group % 8 + per_group + 7) // 8
    merged_tiles = per_group // 8 + tiles
    tile = features if slots_in * merged_tiles * 8 <= 256 else 128
    counts = counts.T
    slots = jnp.transpose(slots, (0, 2, 3, 1))
    hbm = pl.BlockSpec(memory_space=pltpu.HBM)
    return pl.pallas_call(
        functools.partial(exchange, (n_group, n_row, n_col), tile),
        out_shape=jax.ShapeDtypeStruct((1, features, features), jnp.float32),
        in_specs=[hbm, hbm, hbm, hbm],
        out_specs=pl.BlockSpec(memory_space=pltpu.VMEM),
        scratch_shapes=[
            pltpu.SMEM(owner.shape, jnp.int32),
            pltpu.SMEM(counts.shape, jnp.int32),
            pltpu.SMEM(slots.shape, jnp.int32),
            pltpu.VMEM((block_tokens, features), tokens.dtype),
            pltpu.VMEM((2, n_handled, tiles, 8, features), tokens.dtype),
            pltpu.VMEM((n_handled, tiles, 8, features), tokens.dtype),
            pltpu.VMEM((n_handled, merged_tiles, 8, features), tokens.dtype),
            pltpu.VMEM((2, slots_in, merged_tiles, 8, features), tokens.dtype),
            pltpu.SemaphoreType.DMA((4,)),
            pltpu.SemaphoreType.DMA,
            pltpu.SemaphoreType.DMA,
            pltpu.SemaphoreType.DMA,
            pltpu.SemaphoreType.DMA((2, n_handled, max(n_row, n_col))),
            pltpu.SemaphoreType.DMA((2, slots_in)),
        ],
        compiler_params=pltpu.CompilerParams(
            collective_id=0, has_side_effects=True, vmem_limit_bytes=32 * 1024 * 1024
        ),
    )(*[pltpu.with_memory_space_constraint(a, pltpu.HBM) for a in (owner, counts, slots, tokens)])


def solution(mesh):
    return jax.shard_map(
        per_device,
        mesh=mesh,
        in_specs=(P(("expert", "col"), "row"), P(("expert", "col"), None, None, None), P(), P()),
        out_specs=P("expert", "row", "col"),
        check_vma=False,
    )
```

```python
import functools

import jax
import jax.numpy as jnp
from jax import lax
from jax.experimental import pallas as pl
from jax.experimental.pallas import tpu as pltpu
from jax.sharding import PartitionSpec as P

MESH = pl.DeviceIdType.MESH


def each(count, body):
    if count <= 4:
        for i in range(count):
            body(i)
    else:
        pl.loop(0, count)(body)


def wrap(index, count):
    return lax.rem(index + count, count)


def expert_of(owner_ref, group, expert_count):
    found = jnp.int32(0)
    for e in range(expert_count):
        found = jnp.where(owner_ref[e] == group, jnp.int32(e), found)
    return found


def exchange(
    sizes, tile, owner_hbm, counts_hbm, slots_hbm, tokens_hbm, out_ref,
    owner_ref, counts_ref, slots_ref, tokens, picked, landed, merged, relay, buf,
    load_sem, own_sem, pair_send, pair_recv, relay_send, relay_recv, send_sem, recv_sem,
):
    n_group, n_row, n_col = sizes
    block_tokens, features = tokens.shape
    experts, panels = counts_ref.shape
    slot_count = slots_ref.shape[2]
    per_group = panels * slot_count
    _, n_handled, tiles = picked.shape[:3]
    n_pair = n_col // 2
    x, r, c = lax.axis_index("expert"), lax.axis_index("row"), lax.axis_index("col")
    block = x * n_col + c
    parity = c % 2
    partner = c + 1 - 2 * parity

    loads = [
        pltpu.make_async_copy(source, target, load_sem.at[i])
        for i, (source, target) in enumerate(
            [(tokens_hbm, tokens), (slots_hbm, slots_ref), (counts_hbm, counts_ref), (owner_hbm, owner_ref)]
        )
    ]
    for load in loads:
        load.start()

    barrier = pltpu.get_barrier_semaphore()

    def signal(device):
        pl.semaphore_signal(barrier, inc=1, device_id=device, device_id_type=MESH)

    def sender_column(pair):
        return 2 * pair + x % 2

    own = x % 2 == parity

    def greet_lefts(dg):
        for pair in range(n_pair):
            device = (wrap(x + dg, n_group), r, sender_column(pair))
            pl.when(jnp.logical_or(device[0] != x, device[2] != c))(lambda device=device: signal(device))

    def relays(dr):
        return jnp.logical_and(own, wrap(r - dr, n_row) // 2 != c // 2)

    def greet_rights(dg):
        group = wrap(x + dg, n_group)
        pl.when(r != c)(lambda: signal((group, c, sender_column(c // 2))))
        for dr in range(1, n_row):
            pl.when(relays(dr))(lambda dr=dr: signal((group, wrap(r - dr, n_row), c)))

    signal((x, r, partner))
    each(n_group, greet_rights)
    each(n_group, greet_lefts)

    for load in loads[1:]:
        load.wait()
    rows_iota = lax.broadcasted_iota(jnp.int32, (tiles * 8, block_tokens), 0)
    token_iota = lax.broadcasted_iota(jnp.int32, (tiles * 8, block_tokens), 1)

    def first_tile(side):
        return side * (per_group // 8)

    skipped = parity * (per_group % 8)

    def onehot(group):
        e = expert_of(owner_ref, group, experts)
        index = jnp.full((tiles * 8, block_tokens), -1, jnp.int32)
        for k in range(panels):
            count = counts_ref[e, k]
            for j in range(slot_count):
                slot = jnp.where(block * slot_count + j < count, slots_ref[0, e, j, k], jnp.int32(-1))
                index = jnp.where(rows_iota == k * slot_count + j + skipped, slot, index)
        return index == token_iota

    def choose(i):
        return jnp.concatenate([onehot(2 * i), onehot(2 * i + 1)], axis=0).astype(jnp.bfloat16)

    def pick(i, chosen):
        rows = jnp.dot(chosen, tokens[...], preferred_element_type=jnp.float32)
        rows = rows.reshape(2, tiles, 8, features).astype(jnp.bfloat16)
        picked[0, i] = rows[0]
        picked[1, i] = rows[1]

    if n_handled == 1:
        chosen = choose(0)
        loads[0].wait()
        pick(0, chosen)
    else:
        loads[0].wait()
        each(n_handled, lambda i: pick(i, choose(i)))

    sends = 1 + n_handled * (n_col + n_row - 1)

    @pl.when(own)
    def _():
        pl.semaphore_wait(barrier, sends - 1)

    @pl.when(jnp.logical_not(own))
    def _():
        pl.semaphore_wait(barrier, sends)

    pair_copy = pltpu.make_async_remote_copy(
        src_ref=picked.at[1 - parity],
        dst_ref=landed,
        send_sem=pair_send,
        recv_sem=pair_recv,
        device_id=(x, r, partner),
        device_id_type=MESH,
    )
    pair_copy.start()
    merged[...] = jnp.zeros_like(merged)
    merged[:, pl.ds(first_tile(parity), tiles)] = picked[parity]
    pair_copy.wait_recv()
    window = pl.ds(first_tile(1 - parity), tiles)
    merged[:, window] = merged[:, window] + landed[...]

    my_slot = x * n_pair + c // 2

    def handled(di):
        return wrap(x // 2 + di, n_handled)

    relayed = c // 2 != r // 2

    def right_copy(di, dr, by_relay):
        return pltpu.make_async_remote_copy(
            src_ref=merged.at[handled(di)],
            dst_ref=relay.at[x, dr - 1] if by_relay else buf.at[1, my_slot],
            send_sem=send_sem.at[1, di, dr],
            recv_sem=relay_recv.at[x, dr - 1] if by_relay else recv_sem.at[1, my_slot],
            device_id=(2 * handled(di) + parity, wrap(r + dr, n_row), c if by_relay else r),
            device_id_type=MESH,
        )

    def forward_copy(dr, source):
        return pltpu.make_async_remote_copy(
            src_ref=relay.at[source, dr - 1],
            dst_ref=buf.at[1, source * n_pair + c // 2],
            send_sem=relay_send.at[source, dr - 1],
            recv_sem=recv_sem.at[1, source * n_pair + c // 2],
            device_id=(x, r, wrap(r - dr, n_row)),
            device_id_type=MESH,
        )

    def forwards(act):
        for dr in range(1, n_row):
            pl.when(relays(dr))(lambda dr=dr: each(n_group, lambda dg: act(dr, wrap(x + dg, n_group))))

    def forward(dr, source):
        pltpu.make_async_remote_copy(
            src_ref=merged.at[0],
            dst_ref=relay.at[source, dr - 1],
            send_sem=pair_send,
            recv_sem=relay_recv.at[source, dr - 1],
            device_id=(x, r, partner),
            device_id_type=MESH,
        ).wait_recv()
        forward_copy(dr, source).start()

    def left_copy(di, dc):
        return pltpu.make_async_remote_copy(
            src_ref=merged.at[handled(di)],
            dst_ref=buf.at[0, my_slot],
            send_sem=send_sem.at[0, di, dc],
            recv_sem=recv_sem.at[0, my_slot],
            device_id=(2 * handled(di) + parity, r, wrap(c + dc, n_col)),
            device_id_type=MESH,
        )

    def rights(act):
        def some(by_relay):
            def body(di):
                for dr in range(1, n_row):
                    act(right_copy(di, dr, by_relay))
            each(n_handled, body)
        pl.when(relayed)(lambda: some(True))
        pl.when(jnp.logical_not(relayed))(lambda: some(False))

    def lefts(act):
        def body(di):
            for dc in range(1, n_col):
                act(left_copy(di, dc))
            pl.when(2 * handled(di) + parity != x)(lambda: act(left_copy(di, 0)))
        each(n_handled, body)

    own_copy = pltpu.make_async_copy(merged.at[x // 2], buf.at[0, my_slot], own_sem)
    rights(lambda copy: copy.start())
    lefts(lambda copy: copy.start())
    pl.when(own)(own_copy.start)
    forwards(forward)

    def arrived(side, slot):
        pltpu.make_async_remote_copy(
            src_ref=merged.at[0],
            dst_ref=buf.at[side, slot],
            send_sem=pair_send,
            recv_sem=recv_sem.at[side, slot],
            device_id=(x, r, partner),
            device_id_type=MESH,
        ).wait_recv()

    def wait_left(dg):
        group = wrap(x + dg, n_group)
        for pair in range(n_pair):
            sender = sender_column(pair)
            pl.when(jnp.logical_or(group != x, sender != c))(lambda pair=pair: arrived(0, group * n_pair + pair))

    def wait_right(dg):
        for pair in range(n_pair):
            arrived(1, wrap(x + dg, n_group) * n_pair + pair)

    e = expert_of(owner_ref, x, experts)
    total = jnp.int32(0)
    for k in range(panels):
        total = total + counts_ref[e, k]
    scale = 1.0 / jnp.full((1, features), total, jnp.int32).astype(jnp.float32)

    pl.when(own)(own_copy.wait)
    each(n_group, wait_left)

    @pl.when(r != c)
    def _():
        each(n_group, wait_right)

    right_rows = buf[jnp.where(r == c, 0, 1)].reshape(-1, features)
    for t in range(features // tile):
        span = pl.ds(t * tile, tile)
        left_rows = buf[0, :, :, :, span].reshape(-1, tile)
        part = lax.dot_general(left_rows, right_rows, (((0,), (0,)), ((), ())), preferred_element_type=jnp.float32)
        out_ref[0, span, :] = part * scale

    pair_copy.wait_send()
    rights(lambda copy: copy.wait_send())
    lefts(lambda copy: copy.wait_send())
    forwards(lambda dr, source: forward_copy(dr, source).wait_send())


def per_device(tokens, slots, counts, owner):
    n_group, n_row, n_col = lax.axis_size("expert"), lax.axis_size("row"), lax.axis_size("col")
    block_tokens, features = tokens.shape
    panels, slot_count = counts.shape[0], slots.shape[3]
    per_group = panels * slot_count
    n_handled, slots_in = n_group // 2, n_group * n_col // 2
    tiles = (per_group % 8 + per_group + 7) // 8
    merged_tiles = per_group // 8 + tiles
    tile = features if slots_in * merged_tiles * 8 <= 256 else 128
    counts = counts.T
    slots = jnp.transpose(slots, (0, 2, 3, 1))
    hbm = pl.BlockSpec(memory_space=pltpu.HBM)
    return pl.pallas_call(
        functools.partial(exchange, (n_group, n_row, n_col), tile),
        out_shape=jax.ShapeDtypeStruct((1, features, features), jnp.float32),
        in_specs=[hbm, hbm, hbm, hbm],
        out_specs=pl.BlockSpec(memory_space=pltpu.VMEM),
        scratch_shapes=[
            pltpu.SMEM(owner.shape, jnp.int32),
            pltpu.SMEM(counts.shape, jnp.int32),
            pltpu.SMEM(slots.shape, jnp.int32),
            pltpu.VMEM((block_tokens, features), tokens.dtype),
            pltpu.VMEM((2, n_handled, tiles, 8, features), tokens.dtype),
            pltpu.VMEM((n_handled, tiles, 8, features), tokens.dtype),
            pltpu.VMEM((n_handled, merged_tiles, 8, features), tokens.dtype),
            pltpu.VMEM((n_group, n_row - 1, merged_tiles, 8, features), tokens.dtype),
            pltpu.VMEM((2, slots_in, merged_tiles, 8, features), tokens.dtype),
            pltpu.SemaphoreType.DMA((4,)),
            pltpu.SemaphoreType.DMA,
            pltpu.SemaphoreType.DMA,
            pltpu.SemaphoreType.DMA,
            pltpu.SemaphoreType.DMA((n_group, n_row - 1)),
            pltpu.SemaphoreType.DMA((n_group, n_row - 1)),
            pltpu.SemaphoreType.DMA((2, n_handled, max(n_row, n_col))),
            pltpu.SemaphoreType.DMA((2, slots_in)),
        ],
        compiler_params=pltpu.CompilerParams(
            collective_id=0, has_side_effects=True, vmem_limit_bytes=32 * 1024 * 1024
        ),
    )(*[pltpu.with_memory_space_constraint(a, pltpu.HBM) for a in (owner, counts, slots, tokens)])


def solution(mesh):
    return jax.shard_map(
        per_device,
        mesh=mesh,
        in_specs=(P(("expert", "col"), "row"), P(("expert", "col"), None, None, None), P(), P()),
        out_specs=P("expert", "row", "col"),
        check_vma=False,
    )
```
